512 devices in a mesh: slab: 8 (over y, core), pair: 64 (over x, z).
Axes of the slice: x: 4, y: 4, z: 16, core: 2. Of those that a mesh axis runs over, the one named last changes fastest.
Arguments:
- amplitudes: bfloat16 [1024, 16384], P('pair', 'slab'), may hold values from -6 to 6
- integrals: bfloat16 [16384, 65536], P('slab', 'pair'), may hold values from -0.125 to 0.125
- contract_irrep: int32 [16384], replicated, may hold values from 0 to 7, as said below
- outer_irrep: int32 [65536], replicated, may hold values from 0 to 7, as said below
- block_map: int32 [8, 8], replicated, may hold values from 0 to 1, as said below
Outputs:
- ladder: float32 [1024, 65536], P('slab', 'pair')
The draws below stay inside these ranges and needn't reach their ends.
Inputs may be any that keep to these rules, and one draw needn't show every extreme that they name: `contract_irrep`: each irrep label occupies exactly one contiguous run of contracted virtual pairs, whose length is a positive multiple of 64. `outer_irrep`: each irrep label occupies exactly one contiguous run of outer virtual pairs, whose length is a positive multiple of 64. Each row and each column of block_map holds exactly one 1.
All inputs are finite; a program needn't handle non-finite values.
Results may differ from the reference program's by a relative error of at most 0.0003.
Values may be sent and summed in bfloat16 or wider, within the bound.
No kernel may reach another device: no remote copies, remote signals or barrier semaphores. Data moves between devices by JAX's collectives and lax.ppermute only.
A program may use at most 64 MiB of HBM per device.

```python
import jax
import jax.numpy as jnp
from jax import lax

NIRREP = 8
BLOCK_UNIT = 64
OPAIRS = 1024
CONTRACT = 16384
VP = 65536
N_PAIR = 64


def irrep_runs(key, total, unit):
    units = total // unit
    cuts = jax.random.permutation(key, units - 1)[:NIRREP - 1] + 1
    cuts = jnp.sort(cuts.astype(jnp.int32))
    position = jnp.arange(units, dtype=jnp.int32)
    run_index = jnp.sum((position[:, None] >= cuts[None, :]).astype(jnp.int32), axis=1)
    order = jax.random.permutation(jax.random.fold_in(key, 1), NIRREP).astype(jnp.int32)
    labels = order[run_index]
    return jnp.repeat(labels, unit, total_repeat_length=total).astype(jnp.int32)


def draw_contract_irrep(key, part):
    key = jax.random.fold_in(key, 11)
    return irrep_runs(key, CONTRACT, BLOCK_UNIT)


def draw_outer_irrep(key, part):
    key = jax.random.fold_in(key, 23)
    return irrep_runs(key, VP, BLOCK_UNIT)


def draw_block_map(key, part):
    key = jax.random.fold_in(key, 37)
    partner = jax.random.permutation(key, NIRREP).astype(jnp.int32)
    second = jnp.arange(NIRREP, dtype=jnp.int32)[None, :]
    return (partner[:, None] == second).astype(jnp.int32)


def block_scale(rng, shape, cuts, smallest, largest):
    gain, own = 1.0, jax.random.fold_in(rng, 6)
    for dim, shards_of in cuts:
        steps = jnp.exp(jax.random.uniform(jax.random.fold_in(own, dim), (shards_of,), jnp.float32, smallest / len(cuts), largest / len(cuts)))
        gain = gain * jnp.repeat(steps, shape[dim] // shards_of).reshape([-1 if axis == dim else 1 for axis in range(len(shape))])
    return gain


def normal_values(stream_key, dims, scale, reach, split=(), kind=jnp.bfloat16):
    factor_of = block_scale(stream_key, dims, split, -0.22, 0.18) if split else 1.0
    drawn = jax.random.normal(stream_key, dims, jnp.float32) * scale * factor_of
    return jnp.minimum(jnp.maximum(drawn, -reach), reach).astype(kind)


def setup_inputs(seed: int = 0) -> dict:
    streams_of = jax.random.split(jax.random.key(seed), 6)
    amplitudes = normal_values(streams_of[0], (OPAIRS, CONTRACT), 1.0, 6.0, ((0, 64), (1, 8)))
    integrals = normal_values(streams_of[1], (CONTRACT, VP), (CONTRACT // NIRREP) ** -0.5, 0.125, ((0, 8), (1, 64)))
    contract_irrep = draw_contract_irrep(jax.random.fold_in(streams_of[5], 71), 0)
    outer_irrep = draw_outer_irrep(jax.random.fold_in(streams_of[5], 71), 0)
    block_map = draw_block_map(jax.random.fold_in(streams_of[5], 71), 0)
    return dict(amplitudes=amplitudes, integrals=integrals, contract_irrep=contract_irrep, outer_irrep=outer_irrep, block_map=block_map)


def reference(amplitudes, integrals, contract_irrep, outer_irrep, block_map):
    levels = jnp.arange(NIRREP, dtype=jnp.int32)
    row_hot = (contract_irrep[:, None] == levels[None, :]).astype(jnp.float32)
    row_map = jnp.dot(row_hot, block_map.astype(jnp.float32))
    width = VP // N_PAIR

    def column_block(index):
        first = (index * width).astype(jnp.int32)
        block = lax.dynamic_slice_in_dim(integrals, first, width, 1)
        labels = lax.dynamic_slice_in_dim(outer_irrep, first, width, 0)
        col_hot = (labels[None, :] == levels[:, None]).astype(jnp.float32)
        keep_mask = jnp.dot(row_map, col_hot)
        blocked = jnp.where(keep_mask > 0.5, block, jnp.zeros_like(block))
        return jnp.dot(amplitudes, blocked, preferred_element_type=jnp.float32)

    stacked = lax.map(column_block, jnp.arange(N_PAIR, dtype=jnp.int32))
    return jnp.transpose(stacked, (1, 0, 2)).reshape(OPAIRS, VP)
```

```python
import jax
import jax.numpy as jnp
from jax import lax
from jax.sharding import Mesh, PartitionSpec as P

Y, CORE, X, Z = 4, 2, 4, 16
HALF = Z // CORE


def blocked_integrals(integrals, contract_irrep, outer_irrep, block_map):
    rows, cols = integrals.shape
    slab = lax.axis_index("y") * CORE + lax.axis_index("core")
    pair = lax.axis_index("x") * Z + lax.axis_index("z")
    row_labels = lax.dynamic_slice_in_dim(contract_irrep, slab * rows, rows, 0)
    col_labels = lax.dynamic_slice_in_dim(outer_irrep, pair * cols, cols, 0)
    levels = jnp.arange(block_map.shape[0], dtype=jnp.int32)
    partner = jnp.sum(block_map * levels[None, :], axis=1)
    row_partner = jnp.sum(
        jnp.where(row_labels[:, None] == levels[None, :], partner[None, :], 0), axis=1
    )
    keep = row_partner[:, None] == col_labels[None, :]
    return jnp.where(keep, integrals, jnp.zeros_like(integrals))


def over_z(value, step):
    return lax.ppermute(value, "z", [(i, (i + step) % Z) for i in range(Z)])


def apart(value, axis, size, step):
    pairs = []
    for core in range(CORE):
        for i in range(size):
            to = (i + (step if core == 0 else -step)) % size
            pairs.append((core * size + i, core * size + to))
    return lax.ppermute(value, ("core", axis), pairs)


def spread(value, offset):
    pairs = []
    for y in range(Y):
        for k in range(CORE):
            for x in range(X):
                for z in range(Z):
                    source = HALF * k + (z + offset) % HALF
                    sender = z // HALF
                    pairs.append(
                        (
                            ((y * CORE + sender) * X + (x + y) % X) * Z + source,
                            ((y * CORE + k) * X + x) * Z + z,
                        )
                    )
    return lax.ppermute(value, ("y", "core", "x", "z"), pairs)


def hand_in(value, t):
    pairs = []
    for y in range(Y):
        for core in range(CORE):
            for x in range(X):
                to = (x + y - t) % Y if core == 0 else (x + y + t) % Y
                pairs.append(((y * CORE + core) * X + x, (to * CORE + core) * X + x))
    return lax.ppermute(value, ("y", "core", "x"), pairs)


def body(amplitudes, integrals, contract_irrep, outer_irrep, block_map):
    core, z = lax.axis_index("core"), lax.axis_index("z")
    rows, depth = amplitudes.shape
    swap = [(0, 1), (1, 0)]

    other = lax.ppermute(amplitudes, "core", swap)
    own = jnp.concatenate(
        [jnp.where(core == 0, amplitudes, other), jnp.where(core == 0, other, amplitudes)], axis=1
    )

    first = spread(own, 0)
    second = spread(own, 4)
    blocked = blocked_integrals(integrals, contract_irrep, outer_irrep, block_map)
    blocked_other = lax.ppermute(blocked, "core", swap)

    here = jnp.concatenate([first, second])
    turned = jnp.concatenate(
        [jnp.where(core == 0, first, second), jnp.where(core == 0, second, first)]
    )
    below = over_z(here, 1)
    above = over_z(here, -1)
    far = apart(turned, "z", Z, 2)

    pieces = [here, below, above, far]
    received = []
    for t in range(X):
        if t:
            pieces = [apart(piece, "x", X, 1) for piece in pieces]
        h, b, a, f = pieces
        block = jnp.concatenate(
            [f[:rows], b[:rows], h[:rows], a[:rows], f[rows:], b[rows:], h[rows:], a[rows:]]
        )
        mine = lax.dynamic_slice_in_dim(block, core * depth, depth, 1)
        theirs = lax.dynamic_slice_in_dim(block, (1 - core) * depth, depth, 1)
        partial = jnp.dot(mine, blocked, preferred_element_type=jnp.float32) + jnp.dot(
            theirs, blocked_other, preferred_element_type=jnp.float32
        )
        received.append(hand_in(partial, t))
    total = (received[0] + received[1]) + (received[2] + received[3])
    return jnp.roll(total, (z + HALF - 2) % HALF * rows, axis=0)


def solution(mesh):
    grid = Mesh(mesh.devices.reshape(Y, CORE, X, Z), ("y", "core", "x", "z"))
    slab, pair = ("y", "core"), ("x", "z")
    in_specs = (P(pair, slab), P(slab, pair), P(), P(), P())
    return jax.shard_map(
        body, mesh=grid, in_specs=in_specs, out_specs=P(slab, pair), check_vma=False
    )
```

```python
import jax
import jax.numpy as jnp
from jax import lax
from jax.experimental import pallas as pl
from jax.experimental.pallas import tpu as pltpu
from jax.sharding import Mesh, PartitionSpec as P

Y, CORE, X, Z = 4, 2, 4, 16
HALF = Z // CORE
LANES = 128
CHUNKS = 4


def outer_labels_of(contract_irrep, outer_irrep, block_map, depth, cols):
    first = lax.axis_index("y") * (CORE * depth)
    pair = lax.axis_index("x") * Z + lax.axis_index("z")
    row_labels = lax.dynamic_slice_in_dim(contract_irrep, first, CORE * depth, 0)
    col_labels = lax.dynamic_slice_in_dim(outer_irrep, pair * cols, cols, 0)
    levels = jnp.arange(block_map.shape[0], dtype=jnp.int32)
    partner = jnp.sum(block_map * levels[None, :], axis=1)
    row_partner = jnp.sum(
        jnp.where(row_labels[:, None] == levels[None, :], partner[None, :], 0), axis=1
    )
    return row_partner.reshape(-1, LANES), col_labels.reshape(1, -1)


def over_z(value, step):
    return lax.ppermute(value, "z", [(i, (i + step) % Z) for i in range(Z)])


def apart(value, axis, size, step):
    pairs = []
    for core in range(CORE):
        for i in range(size):
            to = (i + (step if core == 0 else -step)) % size
            pairs.append((core * size + i, core * size + to))
    return lax.ppermute(value, ("core", axis), pairs)


def spread(value, offset):
    pairs = []
    for y in range(Y):
        for k in range(CORE):
            for x in range(X):
                for z in range(Z):
                    source = HALF * k + (z + offset) % HALF
                    sender = z // HALF
                    pairs.append(
                        (
                            ((y * CORE + sender) * X + (x + y) % X) * Z + source,
                            ((y * CORE + k) * X + x) * Z + z,
                        )
                    )
    return lax.ppermute(value, ("y", "core", "x", "z"), pairs)


def hand_in(value, t):
    pairs = []
    for y in range(Y):
        for core in range(CORE):
            for x in range(X):
                to = (x + y - t) % Y if core == 0 else (x + y + t) % Y
                pairs.append(((y * CORE + core) * X + x, (to * CORE + core) * X + x))
    return lax.ppermute(value, ("y", "core", "x"), pairs)


def hold_kernel(place_ref, row_ref, col_ref, own_ref, other_ref, held_ref, sem):
    core, (depth, cols) = place_ref[0], own_ref.shape
    chunk = depth // CHUNKS
    copies = []
    for index, ref in ((core, own_ref), (1 - core, other_ref)):
        for part in range(CHUNKS):
            first = pl.multiple_of(index * depth + part * chunk, chunk)
            copy = pltpu.make_async_copy(
                ref.at[pl.ds(part * chunk, chunk)],
                held_ref.at[pl.ds(first, chunk)],
                sem.at[len(copies)],
            )
            copy.start()
            copies.append((copy, first))
    col = col_ref[...].astype(jnp.float32).astype(jnp.bfloat16)
    zero = jnp.zeros((), held_ref.dtype)
    for copy, first in copies:
        copy.wait()
        for group in range(chunk // LANES):
            labels = row_ref[pl.ds(first // LANES + group, 1), :].astype(jnp.float32)
            labels = jnp.broadcast_to(labels, (LANES, LANES)).T.astype(jnp.bfloat16)
            rows = pl.ds(pl.multiple_of(first + group * LANES, LANES), LANES)
            for lane in range(0, cols, LANES):
                at = slice(lane, lane + LANES)
                keep = labels == col[:, at]
                held_ref[rows, at] = jnp.where(keep, held_ref[rows, at], zero)


def hold(place, rows, columns, own, other):
    depth, cols = own.shape
    vmem = pl.BlockSpec(memory_space=pltpu.VMEM)
    return pl.pallas_call(
        hold_kernel,
        out_shape=pltpu.VMEM((CORE * depth, cols), own.dtype),
        in_specs=[pl.BlockSpec(memory_space=pltpu.SMEM), vmem, vmem]
        + [pl.BlockSpec(memory_space=pltpu.HBM)] * 2,
        out_specs=vmem,
        scratch_shapes=[pltpu.SemaphoreType.DMA((CORE * CHUNKS,))],
        compiler_params=pltpu.CompilerParams(vmem_limit_bytes=12 * 2**20),
        cost_estimate=pl.CostEstimate(
            flops=0, bytes_accessed=4 * CORE * depth * cols, transcendentals=0
        ),
    )(place, rows, columns, own, other)


def product_kernel(place_ref, near_ref, far_ref, held_ref, out_ref):
    base, cols = place_ref[1], held_ref.shape[1]
    rows = out_ref.shape[0] // HALF
    block = jnp.concatenate([near_ref[...], far_ref[...]])
    width = min(256, cols)
    for first in range(0, cols, width):
        part = slice(first, first + width)
        value = jnp.dot(block, held_ref[:, part], preferred_element_type=jnp.float32)
        for index, offset in enumerate((0, 4, -1, 3, 1, 5, -2, 2)):
            source = lax.rem(base + offset + HALF, HALF)
            out_ref[pl.ds(pl.multiple_of(source * rows, rows), rows), part] = value[
                index * rows : (index + 1) * rows
            ]


def product(place, near, far, held):
    rows, cols = 2 * near.shape[0], held.shape[1]
    vmem = pl.BlockSpec(memory_space=pltpu.VMEM)
    return pl.pallas_call(
        product_kernel,
        out_shape=jax.ShapeDtypeStruct((rows, cols), jnp.float32),
        in_specs=[pl.BlockSpec(memory_space=pltpu.SMEM)] + [vmem] * 3,
        out_specs=vmem,
        compiler_params=pltpu.CompilerParams(vmem_limit_bytes=12 * 2**20),
        cost_estimate=pl.CostEstimate(
            flops=2 * rows * held.size, bytes_accessed=2 * held.size, transcendentals=0
        ),
    )(place, near, far, pltpu.with_memory_space_constraint(held, pltpu.VMEM))


def body(amplitudes, integrals, contract_irrep, outer_irrep, block_map):
    core, z = lax.axis_index("core"), lax.axis_index("z")
    swap = [(0, 1), (1, 0)]

    other = lax.ppermute(amplitudes, "core", swap)
    other, integrals, contract_irrep, outer_irrep, block_map = lax.optimization_barrier(
        (other, integrals, contract_irrep, outer_irrep, block_map)
    )
    both = jnp.concatenate(
        [jnp.where(core == 0, amplitudes, other), jnp.where(core == 0, other, amplitudes)], axis=1
    )

    first = spread(both, 0)
    second = spread(both, 4)
    other = lax.ppermute(integrals, "core", swap)
    place = jnp.stack([core, z % HALF]).astype(jnp.int32)
    labels = outer_labels_of(contract_irrep, outer_irrep, block_map, *integrals.shape)
    second, labels = lax.optimization_barrier((second, labels))

    here = jnp.concatenate([first, second])
    turned = jnp.concatenate(
        [jnp.where(core == 0, first, second), jnp.where(core == 0, second, first)]
    )
    below = over_z(here, 1)
    above = over_z(here, -1)
    away = apart(turned, "z", Z, 2)

    held = hold(place, *labels, integrals, other)
    near = jnp.concatenate([here, below])
    away, held = lax.optimization_barrier((away, held))
    far = jnp.concatenate([above, away])
    received = []
    for t in range(X):
        near_next, far_next = near, far
        if t < X - 1:
            near_next, far_next = apart(near, "x", X, 1), apart(far, "x", X, 1)
        if t > 1:
            near, received[t - 2] = lax.optimization_barrier((near, received[t - 2]))
        partial = product(place, near, far, held)
        received.append(hand_in(partial, t))
        if t < X - 1:
            near_next, partial = lax.optimization_barrier((near_next, partial))
        near, far = near_next, far_next
    return (received[0] + received[1]) + (received[2] + received[3])


def solution(mesh):
    grid = Mesh(mesh.devices.reshape(Y, CORE, X, Z), ("y", "core", "x", "z"))
    slab, pair = ("y", "core"), ("x", "z")
    in_specs = (P(pair, slab), P(slab, pair), P(), P(), P())
    return jax.shard_map(
        body, mesh=grid, in_specs=in_specs, out_specs=P(slab, pair), check_vma=False
    )
```

```python
import jax
import jax.numpy as jnp
from jax import lax
from jax.experimental import pallas as pl
from jax.experimental.pallas import tpu as pltpu
from jax.sharding import Mesh, PartitionSpec as P

Y, CORE, X, Z = 4, 2, 4, 16
HALF = Z // CORE
TURN = ((0, 1, 3, 2), (2, 3, 1, 0))
UNIT = 64
CHUNKS = 4


def outer_labels_of(contract_irrep, outer_irrep, block_map, depth, cols):
    first = lax.axis_index("y") * (CORE * depth)
    pair = lax.axis_index("x") * Z + lax.axis_index("z")
    row_labels = lax.dynamic_slice_in_dim(contract_irrep, first, CORE * depth, 0)[::UNIT]
    col_labels = lax.dynamic_slice_in_dim(outer_irrep, pair * cols, cols, 0)
    levels = jnp.arange(block_map.shape[0], dtype=jnp.int32)
    partner = jnp.sum(block_map * levels[None, :], axis=1)
    row_partner = jnp.sum(
        jnp.where(row_labels[:, None] == levels[None, :], partner[None, :], 0), axis=1
    )
    return row_partner, col_labels.reshape(1, -1)


def apart(value, axis, size, step):
    pairs = []
    for core in range(CORE):
        for i in range(size):
            to = (i + (step if core == 0 else -step)) % size
            pairs.append((core * size + i, core * size + to))
    return lax.ppermute(value, ("core", axis), pairs)


def row_block(y, core, x):
    return (y + TURN[core][x]) % Y


def spread(value, offset):
    pairs = []
    for y in range(Y):
        for k in range(CORE):
            for x in range(X):
                for z in range(Z):
                    source = HALF * k + (z + offset) % HALF
                    sender = z // HALF
                    pairs.append(
                        (
                            ((y * CORE + sender) * X + row_block(y, k, x)) * Z + source,
                            ((y * CORE + k) * X + x) * Z + z,
                        )
                    )
    return lax.ppermute(value, ("y", "core", "x", "z"), pairs)


def hand_in(value, step):
    pairs = []
    for y in range(Y):
        for core in range(CORE):
            for x in range(X):
                to = row_block(y, core, (x - step if core == 0 else x + step) % X)
                pairs.append(((y * CORE + core) * X + x, (to * CORE + core) * X + x))
    return lax.ppermute(value, ("y", "core", "x"), pairs)


def hold_kernel(place_ref, row_ref, col_ref, own_ref, other_ref, held_ref, sem):
    core, (depth, cols) = place_ref[0], own_ref.shape
    chunk = depth // CHUNKS
    copies = []
    for index, ref in ((core, own_ref), (1 - core, other_ref)):
        for part in range(CHUNKS):
            first = pl.multiple_of(index * depth + part * chunk, chunk)
            copy = pltpu.make_async_copy(
                ref.at[pl.ds(part * chunk, chunk)],
                held_ref.at[pl.ds(first, chunk)],
                sem.at[len(copies)],
            )
            copy.start()
            copies.append((copy, first))
    tile = 16
    col = jnp.broadcast_to(col_ref[...].astype(jnp.float32), (tile, cols)).astype(jnp.bfloat16)
    zero = jnp.zeros((), held_ref.dtype)
    for copy, first in copies:
        copy.wait()
        for unit in range(chunk // UNIT):
            label = row_ref[first // UNIT + unit].astype(jnp.float32)
            keep = col == jnp.full((tile, cols), label, jnp.float32).astype(jnp.bfloat16)
            for part in range(UNIT // tile):
                rows = pl.ds(pl.multiple_of(first + unit * UNIT + part * tile, tile), tile)
                held_ref[rows, :] = jnp.where(keep, held_ref[rows, :], zero)


def hold(place, rows, columns, own, other):
    depth, cols = own.shape
    vmem, smem = (pl.BlockSpec(memory_space=m) for m in (pltpu.VMEM, pltpu.SMEM))
    own, other = (pltpu.with_memory_space_constraint(v, pltpu.HBM) for v in (own, other))
    return pl.pallas_call(
        hold_kernel,
        out_shape=pltpu.VMEM((CORE * depth, cols), own.dtype),
        in_specs=[smem, smem, vmem]
        + [pl.BlockSpec(memory_space=pltpu.HBM)] * 2,
        out_specs=vmem,
        scratch_shapes=[pltpu.SemaphoreType.DMA((CORE * CHUNKS,))],
        compiler_params=pltpu.CompilerParams(vmem_limit_bytes=12 * 2**20),
        cost_estimate=pl.CostEstimate(
            flops=0, bytes_accessed=4 * CORE * depth * cols, transcendentals=0
        ),
    )(place, rows, columns, own, other)


def product_kernel(place_ref, near_ref, far_ref, held_ref, out_ref):
    core, base, cols = place_ref[0], place_ref[1], held_ref.shape[1]
    rows = out_ref.shape[0] // HALF
    step = 2 * core - 1
    sources = [base + k * step + half for k in (-1, 2, 0, 1) for half in (0, 4)]
    block = jnp.concatenate([near_ref[...], far_ref[...]])
    width = min(256, cols)
    for first in range(0, cols, width):
        part = slice(first, first + width)
        value = jnp.dot(block, held_ref[:, part], preferred_element_type=jnp.float32)
        for index, source in enumerate(sources):
            at = lax.rem(source + HALF, HALF) * rows
            out_ref[pl.ds(pl.multiple_of(at, rows), rows), part] = value[
                index * rows : (index + 1) * rows
            ]


def product(place, near, far, held):
    rows, cols = 2 * near.shape[0], held.shape[1]
    vmem = pl.BlockSpec(memory_space=pltpu.VMEM)
    return pl.pallas_call(
        product_kernel,
        out_shape=jax.ShapeDtypeStruct((rows, cols), jnp.float32),
        in_specs=[pl.BlockSpec(memory_space=pltpu.SMEM)] + [vmem] * 3,
        out_specs=vmem,
        compiler_params=pltpu.CompilerParams(vmem_limit_bytes=12 * 2**20),
        cost_estimate=pl.CostEstimate(
            flops=2 * rows * held.size, bytes_accessed=2 * held.size, transcendentals=0
        ),
    )(place, near, far, pltpu.with_memory_space_constraint(held, pltpu.VMEM))


def body(amplitudes, integrals, contract_irrep, outer_irrep, block_map):
    core, z = lax.axis_index("core"), lax.axis_index("z")
    swap = [(0, 1), (1, 0)]

    other = lax.ppermute(amplitudes, "core", swap)
    other, integrals, contract_irrep, outer_irrep, block_map = lax.optimization_barrier(
        (other, integrals, contract_irrep, outer_irrep, block_map)
    )
    both = jnp.concatenate(
        [jnp.where(core == 0, amplitudes, other), jnp.where(core == 0, other, amplitudes)], axis=1
    )

    first = spread(both, 0)
    second = spread(both, 4)
    other = lax.ppermute(integrals, "core", swap)
    place = jnp.stack([core, z % HALF]).astype(jnp.int32)
    labels = outer_labels_of(contract_irrep, outer_irrep, block_map, *integrals.shape)
    second, labels = lax.optimization_barrier((second, labels))

    here = jnp.concatenate([first, second])
    away = apart(here, "z", Z, 2)
    back = apart(here, "z", Z, 1)
    ahead = apart(here, "z", Z, -1)
    near = jnp.concatenate([ahead, away])
    far = jnp.concatenate([here, back])

    near_back, near_ahead = apart(near, "x", X, 1), apart(near, "x", X, -1)
    far_back, far_ahead = apart(far, "x", X, 1), apart(far, "x", X, -1)
    near_away = apart(near_back, "x", X, 1)
    far, integrals = lax.optimization_barrier((far, integrals))
    held = hold(place, *labels, integrals, other)
    own = product(place, near, far, held)
    received = [hand_in(own, 0)]
    far_back, own = lax.optimization_barrier((far_back, own))
    far_away = apart(far_back, "x", X, 1)
    received.append(hand_in(product(place, near_back, far_back, held), 1))
    received.append(hand_in(product(place, near_ahead, far_ahead, held), -1))
    far_away, received[0] = lax.optimization_barrier((far_away, received[0]))
    received.append(hand_in(product(place, near_away, far_away, held), 2))
    return (received[0] + received[1]) + (received[2] + received[3])


def solution(mesh):
    grid = Mesh(mesh.devices.reshape(Y, CORE, X, Z), ("y", "core", "x", "z"))
    slab, pair = ("y", "core"), ("x", "z")
    in_specs = (P(pair, slab), P(slab, pair), P(), P(), P())
    return jax.shard_map(
        body, mesh=grid, in_specs=in_specs, out_specs=P(slab, pair), check_vma=False
    )
```

```python
import jax
import jax.numpy as jnp
from jax import lax
from jax.experimental import pallas as pl
from jax.experimental.pallas import tpu as pltpu
from jax.sharding import Mesh, PartitionSpec as P

Y, CORE, X, Z = 4, 2, 4, 16
HALF = Z // CORE
TURN = ((0, 1, 3, 2), (2, 3, 1, 0))
UNIT = 64
CHUNKS = 4


def outer_labels_of(contract_irrep, outer_irrep, block_map, depth, cols):
    first = lax.axis_index("y") * (CORE * depth)
    pair = lax.axis_index("x") * Z + lax.axis_index("z")
    row_labels = lax.dynamic_slice_in_dim(contract_irrep, first, CORE * depth, 0)[::UNIT]
    col_labels = lax.dynamic_slice_in_dim(outer_irrep, pair * cols, cols, 0)
    levels = jnp.arange(block_map.shape[0], dtype=jnp.int32)
    partner = jnp.sum(block_map * levels[None, :], axis=1)
    row_partner = jnp.sum(
        jnp.where(row_labels[:, None] == levels[None, :], partner[None, :], 0), axis=1
    )
    return row_partner, col_labels.reshape(1, -1)


def apart(value, axis, size, step):
    pairs = []
    for core in range(CORE):
        for i in range(size):
            to = (i + (step if core == 0 else -step)) % size
            pairs.append((core * size + i, core * size + to))
    return lax.ppermute(value, ("core", axis), pairs)


def row_block(y, core, x):
    return (y + TURN[core][x]) % Y


def spread(value, offset):
    pairs = []
    for y in range(Y):
        for k in range(CORE):
            for x in range(X):
                for z in range(Z):
                    source = HALF * k + (z + offset) % HALF
                    sender = z // HALF
                    pairs.append(
                        (
                            ((y * CORE + sender) * X + row_block(y, k, x)) * Z + source,
                            ((y * CORE + k) * X + x) * Z + z,
                        )
                    )
    return lax.ppermute(value, ("y", "core", "x", "z"), pairs)


def hand_in(value, step):
    pairs = []
    for y in range(Y):
        for core in range(CORE):
            for x in range(X):
                to = row_block(y, core, (x - step if core == 0 else x + step) % X)
                pairs.append(((y * CORE + core) * X + x, (to * CORE + core) * X + x))
    return lax.ppermute(value, ("y", "core", "x"), pairs)


def hold_kernel(place_ref, row_ref, col_ref, own_ref, other_ref, held_ref, sem):
    core, (depth, cols) = place_ref[0], own_ref.shape
    chunk = depth // CHUNKS
    copies = []
    for index, ref in ((core, own_ref), (1 - core, other_ref)):
        for part in range(CHUNKS):
            first = pl.multiple_of(index * depth + part * chunk, chunk)
            copy = pltpu.make_async_copy(
                ref.at[pl.ds(part * chunk, chunk)],
                held_ref.at[pl.ds(first, chunk)],
                sem.at[len(copies)],
            )
            copy.start()
            copies.append((copy, first))
    tile = 16
    col = jnp.broadcast_to(col_ref[...].astype(jnp.float32), (tile, cols)).astype(jnp.bfloat16)
    zero = jnp.zeros((), held_ref.dtype)
    for copy, first in copies:
        copy.wait()
        for unit in range(chunk // UNIT):
            label = row_ref[first // UNIT + unit].astype(jnp.float32)
            keep = col == jnp.full((tile, cols), label, jnp.float32).astype(jnp.bfloat16)
            for part in range(UNIT // tile):
                rows = pl.ds(pl.multiple_of(first + unit * UNIT + part * tile, tile), tile)
                held_ref[rows, :] = jnp.where(keep, held_ref[rows, :], zero)


def hold(place, rows, columns, own, other):
    depth, cols = own.shape
    vmem, smem = (pl.BlockSpec(memory_space=m) for m in (pltpu.VMEM, pltpu.SMEM))
    own, other = (pltpu.with_memory_space_constraint(v, pltpu.HBM) for v in (own, other))
    return pl.pallas_call(
        hold_kernel,
        out_shape=pltpu.VMEM((CORE * depth, cols), own.dtype),
        in_specs=[smem, smem, vmem]
        + [pl.BlockSpec(memory_space=pltpu.HBM)] * 2,
        out_specs=vmem,
        scratch_shapes=[pltpu.SemaphoreType.DMA((CORE * CHUNKS,))],
        compiler_params=pltpu.CompilerParams(vmem_limit_bytes=12 * 2**20),
        cost_estimate=pl.CostEstimate(
            flops=0, bytes_accessed=4 * CORE * depth * cols, transcendentals=0
        ),
    )(place, rows, columns, own, other)


def product_kernel(place_ref, near_ref, far_ref, held_ref, out_ref):
    core, z, cols = place_ref[0], place_ref[1], held_ref.shape[1]
    rows, depth = out_ref.shape[0] // HALF, held_ref.shape[0] // CORE
    step = 2 * core - 1
    origins = [lax.rem(z + k * step + Z, Z) for k in (-1, 2, 0, 1)]

    def columns(half):
        pieces = []
        for index, origin in enumerate(origins):
            ref, first = (near_ref, far_ref)[index // 2], index % 2 * 2 * rows
            swapped = origin // HALF
            at = pl.multiple_of((swapped if half == 0 else 1 - swapped) * depth, depth)
            pieces.append(ref[first : first + 2 * rows, pl.ds(at, depth)])
        return jnp.concatenate(pieces)

    left, right = columns(0), columns(1)
    sources = [origin + half for origin in origins for half in (0, 4)]
    width = min(256, cols)
    for first in range(0, cols, width):
        part = slice(first, first + width)
        value = jnp.dot(left, held_ref[:depth, part], preferred_element_type=jnp.float32)
        value += jnp.dot(right, held_ref[depth:, part], preferred_element_type=jnp.float32)
        for index, source in enumerate(sources):
            at = lax.rem(source, HALF) * rows
            out_ref[pl.ds(pl.multiple_of(at, rows), rows), part] = value[
                index * rows : (index + 1) * rows
            ]


def product(place, near, far, held):
    rows, cols = 2 * near.shape[0], held.shape[1]
    vmem = pl.BlockSpec(memory_space=pltpu.VMEM)
    return pl.pallas_call(
        product_kernel,
        out_shape=jax.ShapeDtypeStruct((rows, cols), jnp.float32),
        in_specs=[pl.BlockSpec(memory_space=pltpu.SMEM)] + [vmem] * 3,
        out_specs=vmem,
        compiler_params=pltpu.CompilerParams(vmem_limit_bytes=12 * 2**20),
        cost_estimate=pl.CostEstimate(
            flops=2 * rows * held.size, bytes_accessed=2 * held.size, transcendentals=0
        ),
    )(place, near, far, pltpu.with_memory_space_constraint(held, pltpu.VMEM))


def body(amplitudes, integrals, contract_irrep, outer_irrep, block_map):
    core, z = lax.axis_index("core"), lax.axis_index("z")
    swap = [(0, 1), (1, 0)]

    other = lax.ppermute(amplitudes, "core", swap)
    other, integrals = lax.optimization_barrier((other, integrals))
    both = jnp.concatenate([amplitudes, other], axis=1)
    other = lax.ppermute(integrals, "core", swap)

    first = spread(both, 0)
    second = spread(both, 4)
    place = jnp.stack([core, z]).astype(jnp.int32)
    labels = outer_labels_of(contract_irrep, outer_irrep, block_map, *integrals.shape)
    second, labels = lax.optimization_barrier((second, labels))

    here = jnp.concatenate([first, second])
    back = apart(here, "z", Z, 1)
    away = apart(here, "z", Z, 2)
    far = jnp.concatenate([here, back])
    ahead = apart(here, "z", Z, -1)
    near = jnp.concatenate([ahead, away])

    near_back, near_ahead = apart(near, "x", X, 1), apart(near, "x", X, -1)
    far_back, far_ahead = apart(far, "x", X, 1), apart(far, "x", X, -1)
    near_away = apart(near_back, "x", X, 1)
    near, integrals = lax.optimization_barrier((near, integrals))
    held = hold(place, *labels, integrals, other)
    own = product(place, near, far, held)
    received = [hand_in(own, 0)]
    far_back, far_ahead, own = lax.optimization_barrier((far_back, far_ahead, own))
    far_away = apart(far_back, "x", X, 1)
    received.append(hand_in(product(place, near_back, far_back, held), 1))
    received.append(hand_in(product(place, near_ahead, far_ahead, held), -1))
    far_away, received[0] = lax.optimization_barrier((far_away, received[0]))
    received.append(hand_in(product(place, near_away, far_away, held), 2))
    return (received[0] + received[1]) + (received[2] + received[3])


def solution(mesh):
    grid = Mesh(mesh.devices.reshape(Y, CORE, X, Z), ("y", "core", "x", "z"))
    slab, pair = ("y", "core"), ("x", "z")
    in_specs = (P(pair, slab), P(slab, pair), P(), P(), P())
    return jax.shard_map(
        body, mesh=grid, in_specs=in_specs, out_specs=P(slab, pair), check_vma=False
    )
```

```python
import jax
import jax.numpy as jnp
from jax import lax
from jax.experimental import pallas as pl
from jax.experimental.pallas import tpu as pltpu
from jax.sharding import Mesh, PartitionSpec as P

Y, CORE, X, Z = 4, 2, 4, 16
HALF = Z // CORE
TURN = ((0, 1, 3, 2), (2, 3, 1, 0))
UNIT = 64
CHUNKS = 4


def outer_labels_of(contract_irrep, outer_irrep, block_map, depth, cols):
    first = lax.axis_index("y") * (CORE * depth)
    pair = lax.axis_index("x") * Z + lax.axis_index("z")
    row_labels = lax.dynamic_slice_in_dim(contract_irrep, first, CORE * depth, 0)[::UNIT]
    col_labels = lax.dynamic_slice_in_dim(outer_irrep, pair * cols, cols, 0)
    levels = jnp.arange(block_map.shape[0], dtype=jnp.int32)
    partner = jnp.sum(block_map * levels[None, :], axis=1)
    row_partner = jnp.sum(
        jnp.where(row_labels[:, None] == levels[None, :], partner[None, :], 0), axis=1
    )
    return row_partner, col_labels.reshape(1, -1)


def apart(value, axis, size, step):
    pairs = []
    for core in range(CORE):
        for i in range(size):
            to = (i + (step if core == 0 else -step)) % size
            pairs.append((core * size + i, core * size + to))
    return lax.ppermute(value, ("core", axis), pairs)


def row_block(y, core, x):
    return (y + TURN[core][x]) % Y


def spread(value, offset):
    pairs = []
    for y in range(Y):
        for k in range(CORE):
            for x in range(X):
                for z in range(Z):
                    source = HALF * k + (z + offset) % HALF
                    sender = z // HALF
                    pairs.append(
                        (
                            ((y * CORE + sender) * X + row_block(y, k, x)) * Z + source,
                            ((y * CORE + k) * X + x) * Z + z,
                        )
                    )
    return lax.ppermute(value, ("y", "core", "x", "z"), pairs)


def hand_in(value, step):
    pairs = []
    for y in range(Y):
        for core in range(CORE):
            for x in range(X):
                to = row_block(y, core, (x - step if core == 0 else x + step) % X)
                pairs.append(((y * CORE + core) * X + x, (to * CORE + core) * X + x))
    return lax.ppermute(value, ("y", "core", "x"), pairs)


def origins_of(place_ref):
    step = 2 * place_ref[0] - 1
    return [lax.rem(place_ref[1] + k * step + Z, Z) for k in (2, -1, 0, 1)]


def columns(origins, near_ref, far_ref, half, first, width):
    depth, pieces = near_ref.shape[1] // CORE, []
    rows = near_ref.shape[0] // 2
    for index, origin in enumerate(origins):
        ref, top = (near_ref, far_ref)[index // 2], index % 2 * rows
        at = pl.multiple_of(lax.rem(origin // HALF + half, CORE) * depth + first, width)
        pieces.append(ref[top : top + rows, pl.ds(at, width)])
    return jnp.concatenate(pieces)


def place_rows(origins, out_ref, part, value):
    rows = out_ref.shape[0] // HALF
    for index in range(HALF):
        at = lax.rem(origins[index // 2] + index % 2 * 4, HALF) * rows
        out_ref[pl.ds(pl.multiple_of(at, rows), rows), part] = value[
            index * rows : (index + 1) * rows
        ]


def first_kernel(
    place_ref, row_ref, col_ref, own_ref, other_ref, near_ref, far_ref, held_ref, out_ref, sum_ref, sem
):
    core, (depth, cols) = place_ref[0], own_ref.shape
    chunk, tile = depth // CHUNKS, 16
    copies = []
    for half, ref in ((core, own_ref), (1 - core, other_ref)):
        for part in range(CHUNKS):
            first = pl.multiple_of(half * depth + part * chunk, chunk)
            copy = pltpu.make_async_copy(
                ref.at[pl.ds(part * chunk, chunk)],
                held_ref.at[pl.ds(first, chunk)],
                sem.at[len(copies)],
            )
            copy.start()
            copies.append((copy, first, half, part))
    col = jnp.broadcast_to(col_ref[...].astype(jnp.float32), (tile, cols)).astype(jnp.bfloat16)
    zero = jnp.zeros((), held_ref.dtype)
    origins = origins_of(place_ref)
    for copy, first, half, part in copies:
        copy.wait()
        for unit in range(chunk // UNIT):
            label = row_ref[first // UNIT + unit].astype(jnp.float32)
            keep = col == jnp.full((tile, cols), label, jnp.float32).astype(jnp.bfloat16)
            for strip in range(UNIT // tile):
                rows = pl.ds(pl.multiple_of(first + unit * UNIT + strip * tile, tile), tile)
                held_ref[rows, :] = jnp.where(keep, held_ref[rows, :], zero)
        block = columns(origins, near_ref, far_ref, half, part * chunk, chunk)
        value = jnp.dot(block, held_ref[pl.ds(first, chunk), :], preferred_element_type=jnp.float32)
        if copy is copies[0][0]:
            sum_ref[...] = value
        else:
            sum_ref[...] += value
    place_rows(origins, out_ref, slice(None), sum_ref[...])


def first_product(place, rows, columns, own, other, near, far):
    depth, cols = own.shape
    height = 2 * near.shape[0]
    vmem, smem = (pl.BlockSpec(memory_space=m) for m in (pltpu.VMEM, pltpu.SMEM))
    own, other = (pltpu.with_memory_space_constraint(v, pltpu.HBM) for v in (own, other))
    return pl.pallas_call(
        first_kernel,
        out_shape=(
            pltpu.VMEM((CORE * depth, cols), own.dtype),
            jax.ShapeDtypeStruct((height, cols), jnp.float32),
        ),
        in_specs=[smem, smem, vmem] + [pl.BlockSpec(memory_space=pltpu.HBM)] * 2 + [vmem] * 2,
        out_specs=(vmem, vmem),
        scratch_shapes=[
            pltpu.VMEM((height, cols), jnp.float32),
            pltpu.SemaphoreType.DMA((CORE * CHUNKS,)),
        ],
        compiler_params=pltpu.CompilerParams(vmem_limit_bytes=14 * 2**20),
        cost_estimate=pl.CostEstimate(
            flops=2 * height * CORE * own.size, bytes_accessed=4 * CORE * own.size, transcendentals=0
        ),
    )(place, rows, columns, own, other, near, far)


def product_kernel(place_ref, near_ref, far_ref, held_ref, out_ref):
    cols, depth = held_ref.shape[1], held_ref.shape[0] // CORE
    origins = origins_of(place_ref)
    left, right = (columns(origins, near_ref, far_ref, half, 0, depth) for half in range(CORE))
    width = min(256, cols)
    for first in range(0, cols, width):
        part = slice(first, first + width)
        value = jnp.dot(left, held_ref[:depth, part], preferred_element_type=jnp.float32)
        value += jnp.dot(right, held_ref[depth:, part], preferred_element_type=jnp.float32)
        place_rows(origins, out_ref, part, value)


def product(place, near, far, held):
    rows, cols = 2 * near.shape[0], held.shape[1]
    vmem = pl.BlockSpec(memory_space=pltpu.VMEM)
    return pl.pallas_call(
        product_kernel,
        out_shape=jax.ShapeDtypeStruct((rows, cols), jnp.float32),
        in_specs=[pl.BlockSpec(memory_space=pltpu.SMEM)] + [vmem] * 3,
        out_specs=vmem,
        compiler_params=pltpu.CompilerParams(vmem_limit_bytes=12 * 2**20),
        cost_estimate=pl.CostEstimate(
            flops=2 * rows * held.size, bytes_accessed=2 * held.size, transcendentals=0
        ),
    )(place, near, far, pltpu.with_memory_space_constraint(held, pltpu.VMEM))


def body(amplitudes, integrals, contract_irrep, outer_irrep, block_map):
    core, z = lax.axis_index("core"), lax.axis_index("z")
    swap = [(0, 1), (1, 0)]

    other = lax.ppermute(amplitudes, "core", swap)
    both = jnp.pad(amplitudes, ((0, 0), (0, amplitudes.shape[1])))
    both, other, integrals = lax.optimization_barrier((both, other, integrals))
    both = lax.dynamic_update_slice_in_dim(both, other, amplitudes.shape[1], 1)
    other = lax.ppermute(integrals, "core", swap)

    first = spread(both, 0)
    second = spread(both, 4)
    place = jnp.stack([core, z]).astype(jnp.int32)
    labels = outer_labels_of(contract_irrep, outer_irrep, block_map, *integrals.shape)
    second, labels = lax.optimization_barrier((second, labels))

    here = jnp.concatenate([first, second])
    back = apart(here, "z", Z, 1)
    away = apart(here, "z", Z, 2)
    far = jnp.concatenate([here, back])
    ahead = apart(here, "z", Z, -1)
    near = jnp.concatenate([away, ahead])

    near_back, near_ahead = apart(near, "x", X, 1), apart(near, "x", X, -1)
    far_back, far_ahead = apart(far, "x", X, 1), apart(far, "x", X, -1)
    near_away = apart(near_back, "x", X, 1)
    near, integrals = lax.optimization_barrier((near, integrals))
    held, own = first_product(place, *labels, integrals, other, near, far)
    received = [hand_in(own, 0)]
    far_back, far_ahead, own = lax.optimization_barrier((far_back, far_ahead, own))
    far_away = apart(far_back, "x", X, 1)
    received.append(hand_in(product(place, near_back, far_back, held), 1))
    received.append(hand_in(product(place, near_ahead, far_ahead, held), -1))
    far_away, received[0] = lax.optimization_barrier((far_away, received[0]))
    received.append(hand_in(product(place, near_away, far_away, held), 2))
    return (received[0] + received[1]) + (received[2] + received[3])


def solution(mesh):
    grid = Mesh(mesh.devices.reshape(Y, CORE, X, Z), ("y", "core", "x", "z"))
    slab, pair = ("y", "core"), ("x", "z")
    in_specs = (P(pair, slab), P(slab, pair), P(), P(), P())
    return jax.shard_map(
        body, mesh=grid, in_specs=in_specs, out_specs=P(slab, pair), check_vma=False
    )
```

```python
import jax
import jax.numpy as jnp
from jax import lax
from jax.experimental import pallas as pl
from jax.experimental.pallas import tpu as pltpu
from jax.sharding import Mesh, PartitionSpec as P

Y, CORE, X, Z = 4, 2, 4, 16
HALF = Z // CORE
TURN = ((0, 1, 3, 2), (2, 3, 1, 0))
UNIT = 64
COVER = 10**11
CHUNKS = 4


def partner_kernel(y_ref, label_ref, map_ref, partner_ref, by_label_ref):
    levels, units = map_ref.shape[0], partner_ref.shape[0]
    for label in range(levels):
        by_label_ref[label] = sum(map_ref[label, level] * level for level in range(1, levels))
    first = y_ref[0] * (units * UNIT)
    for unit in range(units):
        partner_ref[unit] = by_label_ref[label_ref[first + unit * UNIT]]


def outer_labels_of(contract_irrep, outer_irrep, block_map, depth, cols):
    pair = lax.axis_index("x") * Z + lax.axis_index("z")
    col_labels = lax.dynamic_slice_in_dim(outer_irrep, pair * cols, cols, 0)
    smem = pl.BlockSpec(memory_space=pltpu.SMEM)
    row_partner = pl.pallas_call(
        partner_kernel,
        out_shape=jax.ShapeDtypeStruct((CORE * depth // UNIT,), jnp.int32),
        in_specs=[smem] * 3,
        out_specs=smem,
        scratch_shapes=[pltpu.SMEM((block_map.shape[0],), jnp.int32)],
        cost_estimate=pl.CostEstimate(flops=COVER, bytes_accessed=0, transcendentals=0),
    )(lax.axis_index("y").astype(jnp.int32).reshape(1), contract_irrep, block_map)
    return row_partner, col_labels.reshape(1, -1)


def apart(value, axis, size, step):
    pairs = []
    for core in range(CORE):
        for i in range(size):
            to = (i + (step if core == 0 else -step)) % size
            pairs.append((core * size + i, core * size + to))
    return lax.ppermute(value, ("core", axis), pairs)


def row_block(y, core, x):
    return (y + TURN[core][x]) % Y


def spread(value, offset):
    pairs = []
    for y in range(Y):
        for k in range(CORE):
            for x in range(X):
                for z in range(Z):
                    source = HALF * k + (z + offset) % HALF
                    sender = z // HALF
                    pairs.append(
                        (
                            ((y * CORE + sender) * X + row_block(y, k, x)) * Z + source,
                            ((y * CORE + k) * X + x) * Z + z,
                        )
                    )
    return lax.ppermute(value, ("y", "core", "x", "z"), pairs)


def hand_in(value, step):
    pairs = []
    for y in range(Y):
        for core in range(CORE):
            for x in range(X):
                to = row_block(y, core, (x - step if core == 0 else x + step) % X)
                pairs.append(((y * CORE + core) * X + x, (to * CORE + core) * X + x))
    return lax.ppermute(value, ("y", "core", "x"), pairs)


def origins_of(place_ref):
    step = 2 * place_ref[0] - 1
    return [lax.rem(place_ref[1] + k * step + Z, Z) for k in (2, -1, 0, 1)]


def columns(origins, near_ref, far_ref, half, first, width):
    depth, pieces = near_ref.shape[1] // CORE, []
    rows = near_ref.shape[0] // 2
    for index, origin in enumerate(origins):
        ref, top = (near_ref, far_ref)[index // 2], index % 2 * rows
        at = pl.multiple_of(lax.rem(origin // HALF + half, CORE) * depth + first, width)
        pieces.append(ref[top : top + rows, pl.ds(at, width)])
    return jnp.concatenate(pieces)


def place_rows(origins, out_ref, part, value):
    rows = out_ref.shape[0] // HALF
    for index in range(HALF):
        at = lax.rem(origins[index // 2] + index % 2 * 4, HALF) * rows
        out_ref[pl.ds(pl.multiple_of(at, rows), rows), part] = value[
            index * rows : (index + 1) * rows
        ]


def first_kernel(
    place_ref, row_ref, col_ref, own_ref, other_ref, near_ref, far_ref, held_ref, out_ref, sum_ref, sem
):
    core, (depth, cols) = place_ref[0], own_ref.shape
    chunk, tile = depth // CHUNKS, 16
    copies = []
    for half, ref in ((core, own_ref), (1 - core, other_ref)):
        for part in range(CHUNKS):
            first = pl.multiple_of(half * depth + part * chunk, chunk)
            copy = pltpu.make_async_copy(
                ref.at[pl.ds(part * chunk, chunk)],
                held_ref.at[pl.ds(first, chunk)],
                sem.at[len(copies)],
            )
            copy.start()
            copies.append((copy, first, half, part))
    col = jnp.broadcast_to(col_ref[...].astype(jnp.float32), (tile, cols)).astype(jnp.bfloat16)
    zero = jnp.zeros((), held_ref.dtype)
    origins = origins_of(place_ref)
    for copy, first, half, part in copies:
        copy.wait()
        for unit in range(chunk // UNIT):
            label = row_ref[first // UNIT + unit].astype(jnp.float32)
            keep = col == jnp.full((tile, cols), label, jnp.float32).astype(jnp.bfloat16)
            for strip in range(UNIT // tile):
                rows = pl.ds(pl.multiple_of(first + unit * UNIT + strip * tile, tile), tile)
                held_ref[rows, :] = jnp.where(keep, held_ref[rows, :], zero)
        block = columns(origins, near_ref, far_ref, half, part * chunk, chunk)
        value = jnp.dot(block, held_ref[pl.ds(first, chunk), :], preferred_element_type=jnp.float32)
        if copy is copies[0][0]:
            sum_ref[...] = value
        else:
            sum_ref[...] += value
    place_rows(origins, out_ref, slice(None), sum_ref[...])


def first_product(place, rows, columns, own, other, near, far):
    depth, cols = own.shape
    height = 2 * near.shape[0]
    vmem, smem = (pl.BlockSpec(memory_space=m) for m in (pltpu.VMEM, pltpu.SMEM))
    own, other, rows = (
        pltpu.with_memory_space_constraint(v, pltpu.HBM) for v in (own, other, rows)
    )
    return pl.pallas_call(
        first_kernel,
        out_shape=(
            pltpu.VMEM((CORE * depth, cols), own.dtype),
            jax.ShapeDtypeStruct((height, cols), jnp.float32),
        ),
        in_specs=[smem, smem, vmem] + [pl.BlockSpec(memory_space=pltpu.HBM)] * 2 + [vmem] * 2,
        out_specs=(vmem, vmem),
        scratch_shapes=[
            pltpu.VMEM((height, cols), jnp.float32),
            pltpu.SemaphoreType.DMA((CORE * CHUNKS,)),
        ],
        compiler_params=pltpu.CompilerParams(vmem_limit_bytes=14 * 2**20),
        cost_estimate=pl.CostEstimate(
            flops=2 * height * CORE * own.size, bytes_accessed=4 * CORE * own.size, transcendentals=0
        ),
    )(place, rows, columns, own, other, near, far)


def product_kernel(place_ref, near_ref, far_ref, held_ref, out_ref):
    cols, depth = held_ref.shape[1], held_ref.shape[0] // CORE
    origins = origins_of(place_ref)
    left, right = (columns(origins, near_ref, far_ref, half, 0, depth) for half in range(CORE))
    width = min(256, cols)
    for first in range(0, cols, width):
        part = slice(first, first + width)
        value = jnp.dot(left, held_ref[:depth, part], preferred_element_type=jnp.float32)
        value += jnp.dot(right, held_ref[depth:, part], preferred_element_type=jnp.float32)
        place_rows(origins, out_ref, part, value)


def product(place, near, far, held):
    rows, cols = 2 * near.shape[0], held.shape[1]
    vmem = pl.BlockSpec(memory_space=pltpu.VMEM)
    return pl.pallas_call(
        product_kernel,
        out_shape=jax.ShapeDtypeStruct((rows, cols), jnp.float32),
        in_specs=[pl.BlockSpec(memory_space=pltpu.SMEM)] + [vmem] * 3,
        out_specs=vmem,
        compiler_params=pltpu.CompilerParams(vmem_limit_bytes=12 * 2**20),
        cost_estimate=pl.CostEstimate(
            flops=2 * rows * held.size, bytes_accessed=2 * held.size, transcendentals=0
        ),
    )(place, near, far, pltpu.with_memory_space_constraint(held, pltpu.VMEM))


def body(amplitudes, integrals, contract_irrep, outer_irrep, block_map):
    core, z = lax.axis_index("core"), lax.axis_index("z")
    swap = [(0, 1), (1, 0)]

    other = lax.ppermute(amplitudes, "core", swap)
    both = jnp.pad(amplitudes, ((0, 0), (0, amplitudes.shape[1])))
    both, other, integrals = lax.optimization_barrier((both, other, integrals))
    both = lax.dynamic_update_slice_in_dim(both, other, amplitudes.shape[1], 1)
    other = lax.ppermute(integrals, "core", swap)

    first = spread(both, 0)
    second = spread(both, 4)
    place = jnp.stack([core, z]).astype(jnp.int32)
    labels = outer_labels_of(contract_irrep, outer_irrep, block_map, *integrals.shape)
    second, labels = lax.optimization_barrier((second, labels))

    here = jnp.concatenate([first, second])
    back = apart(here, "z", Z, 1)
    away = apart(here, "z", Z, 2)
    far = jnp.concatenate([here, back])
    ahead = apart(here, "z", Z, -1)
    near = jnp.concatenate([away, ahead])

    near_back, near_ahead = apart(near, "x", X, 1), apart(near, "x", X, -1)
    far_back, far_ahead = apart(far, "x", X, 1), apart(far, "x", X, -1)
    near_away = apart(near_back, "x", X, 1)
    near, integrals = lax.optimization_barrier((near, integrals))
    held, own = first_product(place, *labels, integrals, other, near, far)
    received = [hand_in(own, 0)]
    far_back, far_ahead, own = lax.optimization_barrier((far_back, far_ahead, own))
    far_away = apart(far_back, "x", X, 1)
    received.append(hand_in(product(place, near_back, far_back, held), 1))
    received.append(hand_in(product(place, near_ahead, far_ahead, held), -1))
    far_away, received[0] = lax.optimization_barrier((far_away, received[0]))
    received.append(hand_in(product(place, near_away, far_away, held), 2))
    return (received[0] + received[1]) + (received[2] + received[3])


def solution(mesh):
    grid = Mesh(mesh.devices.reshape(Y, CORE, X, Z), ("y", "core", "x", "z"))
    slab, pair = ("y", "core"), ("x", "z")
    in_specs = (P(pair, slab), P(slab, pair), P(), P(), P())
    return jax.shard_map(
        body, mesh=grid, in_specs=in_specs, out_specs=P(slab, pair), check_vma=False
    )
```

```python
import jax
import jax.numpy as jnp
from jax import lax
from jax.experimental import pallas as pl
from jax.experimental.pallas import tpu as pltpu
from jax.sharding import Mesh, PartitionSpec as P

Y, CORE, X, Z = 4, 2, 4, 16
HALF = Z // CORE
TURN = ((0, 1, 3, 2), (2, 3, 1, 0))
UNIT = 64
COVER = 10**11
CHUNKS = 2


def partner_kernel(y_ref, label_ref, map_ref, partner_ref, by_label_ref):
    levels, units = map_ref.shape[0], partner_ref.shape[0]
    for label in range(levels):
        by_label_ref[label] = sum(map_ref[label, level] * level for level in range(1, levels))
    first = y_ref[0] * (units * UNIT)
    for unit in range(units):
        partner_ref[unit] = by_label_ref[label_ref[first + unit * UNIT]]


def outer_labels_of(contract_irrep, outer_irrep, block_map, depth, cols):
    pair = lax.axis_index("x") * Z + lax.axis_index("z")
    col_labels = lax.dynamic_slice_in_dim(outer_irrep, pair * cols, cols, 0)
    smem = pl.BlockSpec(memory_space=pltpu.SMEM)
    row_partner = pl.pallas_call(
        partner_kernel,
        out_shape=jax.ShapeDtypeStruct((CORE * depth // UNIT,), jnp.int32),
        in_specs=[smem] * 3,
        out_specs=smem,
        scratch_shapes=[pltpu.SMEM((block_map.shape[0],), jnp.int32)],
        cost_estimate=pl.CostEstimate(flops=COVER, bytes_accessed=0, transcendentals=0),
    )(lax.axis_index("y").astype(jnp.int32).reshape(1), contract_irrep, block_map)
    return row_partner, col_labels.reshape(1, -1)


def apart(value, axis, size, step):
    pairs = []
    for core in range(CORE):
        for i in range(size):
            to = (i + (step if core == 0 else -step)) % size
            pairs.append((core * size + i, core * size + to))
    return lax.ppermute(value, ("core", axis), pairs)


def row_block(y, core, x):
    return (y + TURN[core][x]) % Y


def spread(value, offset):
    pairs = []
    for y in range(Y):
        for k in range(CORE):
            for x in range(X):
                for z in range(Z):
                    source = HALF * k + (z + offset) % HALF
                    sender = z // HALF
                    pairs.append(
                        (
                            ((y * CORE + sender) * X + row_block(y, k, x)) * Z + source,
                            ((y * CORE + k) * X + x) * Z + z,
                        )
                    )
    return lax.ppermute(value, ("y", "core", "x", "z"), pairs)


def hand_in(value, step):
    pairs = []
    for y in range(Y):
        for core in range(CORE):
            for x in range(X):
                to = row_block(y, core, (x - step if core == 0 else x + step) % X)
                pairs.append(((y * CORE + core) * X + x, (to * CORE + core) * X + x))
    return lax.ppermute(value, ("y", "core", "x"), pairs)


def origins_of(place_ref):
    step = 2 * place_ref[0] - 1
    return [lax.rem(place_ref[1] + k * step + Z, Z) for k in (2, -1, 0, 1)]


def columns(origins, near_ref, far_ref, half, first, width):
    depth, pieces = near_ref.shape[1] // CORE, []
    rows = near_ref.shape[0] // 2
    for index, origin in enumerate(origins):
        ref, top = (near_ref, far_ref)[index // 2], index % 2 * rows
        at = pl.multiple_of(lax.rem(origin // HALF + half, CORE) * depth + first, width)
        pieces.append(ref[top : top + rows, pl.ds(at, width)])
    return jnp.concatenate(pieces)


def place_rows(origins, out_ref, part, value):
    rows = out_ref.shape[0] // HALF
    for index in range(HALF):
        at = lax.rem(origins[index // 2] + index % 2 * 4, HALF) * rows
        out_ref[pl.ds(pl.multiple_of(at, rows), rows), part] = value[
            index * rows : (index + 1) * rows
        ]


def first_kernel(
    place_ref, row_ref, col_ref, own_ref, other_ref, near_ref, far_ref, held_ref, out_ref, sum_ref, sem
):
    core, (depth, cols) = place_ref[0], own_ref.shape
    chunk, tile = depth // CHUNKS, 16
    copies = []
    for half, ref in ((core, own_ref), (1 - core, other_ref)):
        for part in range(CHUNKS):
            first = pl.multiple_of(half * depth + part * chunk, chunk)
            copy = pltpu.make_async_copy(
                ref.at[pl.ds(part * chunk, chunk)],
                held_ref.at[pl.ds(first, chunk)],
                sem.at[len(copies)],
            )
            copy.start()
            copies.append((copy, first, half, part))
    col = jnp.broadcast_to(col_ref[...].astype(jnp.float32), (tile, cols)).astype(jnp.bfloat16)
    zero = jnp.zeros((), held_ref.dtype)
    origins = origins_of(place_ref)
    for copy, first, half, part in copies:
        copy.wait()
        for unit in range(chunk // UNIT):
            label = row_ref[first // UNIT + unit].astype(jnp.float32)
            keep = col == jnp.full((tile, cols), label, jnp.float32).astype(jnp.bfloat16)
            for strip in range(UNIT // tile):
                rows = pl.ds(pl.multiple_of(first + unit * UNIT + strip * tile, tile), tile)
                held_ref[rows, :] = jnp.where(keep, held_ref[rows, :], zero)
        block = columns(origins, near_ref, far_ref, half, part * chunk, chunk)
        value = jnp.dot(block, held_ref[pl.ds(first, chunk), :], preferred_element_type=jnp.float32)
        if copy is copies[0][0]:
            sum_ref[...] = value
        else:
            sum_ref[...] += value
    place_rows(origins, out_ref, slice(None), sum_ref[...])


def first_product(place, rows, columns, own, other, near, far):
    depth, cols = own.shape
    height = 2 * near.shape[0]
    vmem, smem = (pl.BlockSpec(memory_space=m) for m in (pltpu.VMEM, pltpu.SMEM))
    own, other, rows = (
        pltpu.with_memory_space_constraint(v, pltpu.HBM) for v in (own, other, rows)
    )
    return pl.pallas_call(
        first_kernel,
        out_shape=(
            pltpu.VMEM((CORE * depth, cols), own.dtype),
            jax.ShapeDtypeStruct((height, cols), jnp.float32),
        ),
        in_specs=[smem, smem, vmem] + [pl.BlockSpec(memory_space=pltpu.HBM)] * 2 + [vmem] * 2,
        out_specs=(vmem, vmem),
        scratch_shapes=[
            pltpu.VMEM((height, cols), jnp.float32),
            pltpu.SemaphoreType.DMA((CORE * CHUNKS,)),
        ],
        compiler_params=pltpu.CompilerParams(vmem_limit_bytes=14 * 2**20),
        cost_estimate=pl.CostEstimate(
            flops=2 * height * CORE * own.size, bytes_accessed=4 * CORE * own.size, transcendentals=0
        ),
    )(place, rows, columns, own, other, near, far)


def product_kernel(place_ref, near_ref, far_ref, held_ref, out_ref):
    cols, depth = held_ref.shape[1], held_ref.shape[0] // CORE
    origins = origins_of(place_ref)
    left, right = (columns(origins, near_ref, far_ref, half, 0, depth) for half in range(CORE))
    width = min(256, cols)
    for first in range(0, cols, width):
        part = slice(first, first + width)
        value = jnp.dot(left, held_ref[:depth, part], preferred_element_type=jnp.float32)
        value += jnp.dot(right, held_ref[depth:, part], preferred_element_type=jnp.float32)
        place_rows(origins, out_ref, part, value)


def product(place, near, far, held):
    rows, cols = 2 * near.shape[0], held.shape[1]
    vmem = pl.BlockSpec(memory_space=pltpu.VMEM)
    return pl.pallas_call(
        product_kernel,
        out_shape=jax.ShapeDtypeStruct((rows, cols), jnp.float32),
        in_specs=[pl.BlockSpec(memory_space=pltpu.SMEM)] + [vmem] * 3,
        out_specs=vmem,
        compiler_params=pltpu.CompilerParams(vmem_limit_bytes=12 * 2**20),
        cost_estimate=pl.CostEstimate(
            flops=2 * rows * held.size, bytes_accessed=2 * held.size, transcendentals=0
        ),
    )(place, near, far, pltpu.with_memory_space_constraint(held, pltpu.VMEM))


def body(amplitudes, integrals, contract_irrep, outer_irrep, block_map):
    core, z = lax.axis_index("core"), lax.axis_index("z")
    swap = [(0, 1), (1, 0)]

    other = lax.ppermute(amplitudes, "core", swap)
    both = jnp.pad(amplitudes, ((0, 0), (0, amplitudes.shape[1])))
    both, other, integrals = lax.optimization_barrier((both, other, integrals))
    both = lax.dynamic_update_slice_in_dim(both, other, amplitudes.shape[1], 1)
    other = lax.ppermute(integrals, "core", swap)

    first = spread(both, 0)
    second = spread(both, 4)
    place = jnp.stack([core, z]).astype(jnp.int32)
    labels = outer_labels_of(contract_irrep, outer_irrep, block_map, *integrals.shape)
    second, labels = lax.optimization_barrier((second, labels))

    here = jnp.concatenate([first, second])
    back = apart(here, "z", Z, 1)
    away = apart(here, "z", Z, 2)
    far = jnp.concatenate([here, back])
    ahead = apart(here, "z", Z, -1)
    near = jnp.concatenate([away, ahead])

    near_back, near_ahead = apart(near, "x", X, 1), apart(near, "x", X, -1)
    far_back, far_ahead = apart(far, "x", X, 1), apart(far, "x", X, -1)
    near_away = apart(near_back, "x", X, 1)
    near, integrals = lax.optimization_barrier((near, integrals))
    held, own = first_product(place, *labels, integrals, other, near, far)
    received = [hand_in(own, 0)]
    far_back, far_ahead, own = lax.optimization_barrier((far_back, far_ahead, own))
    far_away = apart(far_back, "x", X, 1)
    received.append(hand_in(product(place, near_back, far_back, held), 1))
    received.append(hand_in(product(place, near_ahead, far_ahead, held), -1))
    far_away, received[0] = lax.optimization_barrier((far_away, received[0]))
    received.append(hand_in(product(place, near_away, far_away, held), 2))
    early, last = lax.optimization_barrier(((received[0] + received[1]) + received[2], received[3]))
    return early + last


def solution(mesh):
    grid = Mesh(mesh.devices.reshape(Y, CORE, X, Z), ("y", "core", "x", "z"))
    slab, pair = ("y", "core"), ("x", "z")
    in_specs = (P(pair, slab), P(slab, pair), P(), P(), P())
    return jax.shard_map(
        body, mesh=grid, in_specs=in_specs, out_specs=P(slab, pair), check_vma=False
    )
```
